512 devices in a mesh: pipe: 16 (over z_lo, y), ctx: 16 (over x, z_hi), tp: 2 (over core).
Axes of the slice: x: 4, y: 4, z: 16 (z_hi: 4, z_lo: 4; z = z_hi * 4 + z_lo), core: 2. Of those that a mesh axis runs over, the one named last changes fastest.
Arguments:
- pending_activity: bfloat16 [16, 1, 1024, 8192], P('pipe', None, 'ctx', 'tp'), may hold values from -6 to 6
- entry_rescale_vector: bfloat16 [16, 1, 8192], P('pipe', None, 'tp'), may hold values from 0.099609375 to 1.8984375
- probe_lifting_matrices: bfloat16 [16, 1, 64, 128, 64], P('pipe', None, 'tp')
- lookup_lifting_matrices: bfloat16 [16, 1, 64, 128, 64], P('pipe', None, 'tp')
- usable_extents: int32 [16, 1], P('pipe'), may hold values from 256 to 1024, as said below
- payoff_readout_vector: bfloat16 [8192], P('tp'), may hold values from -0.0625 to 0.0625
Outputs:
- handed: bfloat16 [16, 1, 1024, 8192], P('pipe', None, 'ctx', 'tp')
- scores: float32 [16, 1], P('pipe')
The draws below stay inside these ranges and needn't reach their ends.
Inputs may be any that keep to these rules, and one draw needn't show every extreme that they name: `usable_extents`: in some section every trace is valid at all 1024 positions.
All inputs are finite; a program needn't handle non-finite values.
Results may differ from the reference program's by a relative error of at most 0.007.
Values may be sent and summed in bfloat16 or wider, within the bound.
No kernel may reach another device: no remote copies, remote signals or barrier semaphores. Data moves between devices by JAX's collectives and lax.ppermute only.
A program may use at most 128 MiB of HBM per device.

```python
import math
import jax
import jax.numpy as jnp
from jax import lax

EMBED_DIMENSION = 8192
HEADS = 64
HEAD = 128
FEAT_HALF = 64
LAYERS = 1
SEGMENT_SEQUENCES = 1
GROUP = 64
DEPTH_SEGMENTS = 16
SEQUENCE_LENGTH = 1024


def feature_weights(key, scale):
    base = jax.random.normal(key, (DEPTH_SEGMENTS, LAYERS, HEADS, HEAD, FEAT_HALF), jnp.float32) * HEAD ** (-0.5) * 2.0
    factor = jnp.exp(jax.random.uniform(jax.random.fold_in(key, 11), (DEPTH_SEGMENTS, LAYERS, HEADS, 1, 1), jnp.float32, 0.0, scale))
    return (base * factor).astype(jnp.bfloat16)


def draw_probe_lifting_matrices(key, part):
    key = jax.random.fold_in(key, 1)
    return feature_weights(key, math.log(2.0))


def draw_lookup_lifting_matrices(key, part):
    key = jax.random.fold_in(key, 2)
    return feature_weights(key, math.log(2.0))


def draw_usable_extents(key, part):
    key = jax.random.fold_in(key, 3)
    base = jax.random.randint(key, (DEPTH_SEGMENTS, SEGMENT_SEQUENCES), SEQUENCE_LENGTH // 4, SEQUENCE_LENGTH + 1)
    chosen = jax.random.randint(jax.random.fold_in(key, 5), (1, 1), 0, DEPTH_SEGMENTS)
    section_ids = jnp.arange(DEPTH_SEGMENTS, dtype=jnp.int32)[:, None]
    return jnp.where(section_ids == chosen, SEQUENCE_LENGTH, base).astype(jnp.int32)


def block_levels(stream_key, extent, split, low, high):
    def one(dim, shards_of):
        heights = jax.random.uniform(jax.random.fold_in(jax.random.fold_in(stream_key, 6), dim), (shards_of,), jnp.float32, low / len(split), high / len(split))
        return jnp.repeat(jnp.exp(heights), extent[dim] // shards_of).reshape((-1,) + (1,) * (len(extent) - dim - 1))

    level = one(*split[0])
    for cut in split[1:]:
        level = level * one(*cut)
    return level


def noise(rng, extent, width, bound, cuts=(), kind=jnp.bfloat16):
    entries = width * jax.random.normal(rng, extent, jnp.float32)
    if cuts:
        entries = entries * block_levels(rng, extent, cuts, -0.22, 0.18)
    return jnp.clip(entries, -bound, bound).astype(kind)


def setup_inputs(seed: int = 0) -> dict:
    arg_keys = jax.random.split(jax.random.key(seed), 7)
    pending_activity = noise(arg_keys[0], (DEPTH_SEGMENTS, SEGMENT_SEQUENCES, SEQUENCE_LENGTH, EMBED_DIMENSION), 1.0, 6.0, ((0, 16), (2, 16), (3, 2)))
    entry_rescale_vector = jnp.clip(1.0 + 0.18 * jax.random.normal(arg_keys[1], (DEPTH_SEGMENTS, LAYERS, EMBED_DIMENSION), jnp.float32), 0.099609375, 1.8984375).astype(jnp.bfloat16)
    probe_lifting_matrices = draw_probe_lifting_matrices(jax.random.fold_in(arg_keys[6], 71), 0)
    lookup_lifting_matrices = draw_lookup_lifting_matrices(jax.random.fold_in(arg_keys[6], 71), 0)
    usable_extents = draw_usable_extents(jax.random.fold_in(arg_keys[6], 71), 0)
    payoff_readout_vector = noise(arg_keys[5], (EMBED_DIMENSION,), EMBED_DIMENSION ** -0.5, 0.0625, ((0, 2),))
    return dict(pending_activity=pending_activity, entry_rescale_vector=entry_rescale_vector, probe_lifting_matrices=probe_lifting_matrices, lookup_lifting_matrices=lookup_lifting_matrices, usable_extents=usable_extents, payoff_readout_vector=payoff_readout_vector)


eps_norm = 1e-05

def feature(u):
    return jnp.concatenate([jax.nn.softmax(u, axis=-1), jax.nn.softmax(-u, axis=-1)], axis=-1)

def layer(final_results, gain, fquery, fkey, length):
    yf = final_results.astype(jnp.float32)
    normed = (yf * lax.rsqrt(lax.optimization_barrier(jnp.mean(yf * yf, axis=-1, keepdims=True)) + eps_norm) * gain.astype(jnp.float32)).astype(jnp.bfloat16)
    blocks = SEQUENCE_LENGTH // GROUP
    position = jnp.arange(SEQUENCE_LENGTH, dtype=jnp.int32)
    valid = (position[None, :] < length[:, None]).astype(jnp.float32)
    heads_in = normed.reshape(SEGMENT_SEQUENCES, blocks, GROUP, HEADS, HEAD).transpose(1, 0, 2, 3, 4)
    rows_in = yf.reshape(SEGMENT_SEQUENCES, blocks, GROUP, EMBED_DIMENSION).transpose(1, 0, 2, 3)
    valid_blocks = valid.reshape(SEGMENT_SEQUENCES, blocks, GROUP).transpose(1, 0, 2)
    causal = (jnp.arange(GROUP)[:, None] >= jnp.arange(GROUP)[None, :]).astype(jnp.float32)
    fq = fquery.astype(jnp.float32)
    fk = fkey.astype(jnp.float32)

    def step(carry, inputs):
        state, zsum = carry
        values, rows, mask = inputs
        vf = values.astype(jnp.float32)
        query = feature(jnp.einsum('bchd,hdf->bchf', vf, fq)).astype(jnp.bfloat16).astype(jnp.float32)
        keys = (feature(jnp.einsum('bchd,hdf->bchf', vf, fk)) * mask[:, :, None, None]).astype(jnp.bfloat16).astype(jnp.float32)
        scores_in = jnp.einsum('bchf,bshf->bhcs', query, keys) * causal
        den = lax.optimization_barrier(jnp.sum(scores_in, axis=-1)).transpose(0, 2, 1)
        den = den + jnp.einsum('bchf,bhf->bch', query, zsum, precision=lax.Precision.HIGHEST)
        weights = scores_in.astype(jnp.bfloat16).astype(jnp.float32)
        num = jnp.einsum('bhcs,bshe->bche', weights, vf)
        num = num + jnp.einsum('bchf,bhfe->bche', query, state, precision=lax.Precision.HIGHEST)
        attn = num / den[..., None]
        out = ((rows + attn.reshape(SEGMENT_SEQUENCES, GROUP, EMBED_DIMENSION)) * mask[:, :, None]).astype(jnp.bfloat16)
        state = state + jnp.einsum('bchf,bche->bhfe', keys, vf)
        zsum = zsum + lax.optimization_barrier(jnp.sum(keys, axis=1))
        return ((state, zsum), out)
    init = (jnp.zeros((SEGMENT_SEQUENCES, HEADS, 2 * FEAT_HALF, HEAD), jnp.float32), jnp.zeros((SEGMENT_SEQUENCES, HEADS, 2 * FEAT_HALF), jnp.float32))
    carry, outs = lax.scan(step, init, (heads_in, rows_in, valid_blocks))
    return outs.transpose(1, 0, 2, 3).reshape(SEGMENT_SEQUENCES, SEQUENCE_LENGTH, EMBED_DIMENSION)

def readout_row(final_results, length, weight):
    rows = final_results[jnp.arange(SEGMENT_SEQUENCES), length - 1].astype(jnp.float32)
    num = lax.optimization_barrier(jnp.sum(rows * weight.astype(jnp.float32), axis=-1))
    return num * lax.rsqrt(lax.optimization_barrier(jnp.mean(rows * rows, axis=-1)) + eps_norm)

def reference(pending_activity, entry_rescale_vector, probe_lifting_matrices, lookup_lifting_matrices, usable_extents, payoff_readout_vector):
    outs = []
    found = []
    for segment_ordinal in range(DEPTH_SEGMENTS):
        final_results = pending_activity[segment_ordinal]
        for level in range(LAYERS):
            final_results = layer(final_results, entry_rescale_vector[segment_ordinal, level], probe_lifting_matrices[segment_ordinal, level], lookup_lifting_matrices[segment_ordinal, level], usable_extents[segment_ordinal])
        outs.append(final_results)
        found.append(readout_row(final_results, usable_extents[segment_ordinal], payoff_readout_vector))
    handed = jnp.roll(jnp.stack(outs), 1, axis=0)
    return (handed, jnp.stack(found))
```

```python
import functools

import jax
import jax.numpy as jnp
from jax import lax
from jax.experimental import pallas as pl
from jax.experimental.pallas import tpu as pltpu
from jax.sharding import PartitionSpec as P

EMBED_DIMENSION = 8192
HEAD = 128
CHUNK = 256

eps_norm = 1e-05


def squares_kernel(y_ref, out_ref):
    total = jnp.zeros((y_ref.shape[0], 128), jnp.float32)
    for j in range(0, y_ref.shape[1], 128):
        part = y_ref[:, j : j + 128].astype(jnp.float32)
        total = total + part * part
    out_ref[...] = jnp.sum(total.T, axis=0, keepdims=True)


def norm_kernel(y_ref, squares_ref, gain_ref, out_ref):
    pieces, group, wide = out_ref.shape
    scale = lax.rsqrt(squares_ref[...] / EMBED_DIMENSION + eps_norm)
    scale = jnp.broadcast_to(scale, (128, group)).T
    for j in range(pieces):
        for i in range(0, wide, 128):
            at = j * wide + i
            part = y_ref[:, at : at + 128].astype(jnp.float32) * scale
            part = part * gain_ref[:, at : at + 128].astype(jnp.float32)
            out_ref[j, :, i : i + 128] = part.astype(jnp.bfloat16)


def feature(u):
    up = jnp.exp(u - jnp.max(u, axis=0, keepdims=True))
    down = jnp.exp(jnp.min(u, axis=0, keepdims=True) - u)
    up = up / jnp.sum(up, axis=0, keepdims=True)
    down = down / jnp.sum(down, axis=0, keepdims=True)
    return jnp.concatenate([up, down], axis=0)


def dot(a, b, dims):
    return lax.dot_general(a, b, (dims, ((), ())), preferred_element_type=jnp.float32)


def heads_kernel(where_ref, v_ref, probe_ref, lookup_ref, out_ref):
    length = where_ref[1]
    positions = v_ref.shape[0]
    causal = lax.broadcasted_iota(jnp.int32, (CHUNK, CHUNK), 0) >= lax.broadcasted_iota(
        jnp.int32, (CHUNK, CHUNK), 1
    )
    valid = (
        lax.broadcasted_iota(jnp.int32, (1, positions), 1) < length
    ).astype(jnp.float32)
    ones = jnp.ones((CHUNK, HEAD), jnp.bfloat16)
    for h in range(probe_ref.shape[0]):
        cols = slice(h * HEAD, (h + 1) * HEAD)
        v = v_ref[:, cols]
        query = feature(dot(probe_ref[h], v, ((0,), (1,)))).astype(jnp.bfloat16)
        keys = (feature(dot(lookup_ref[h], v, ((0,), (1,)))) * valid).astype(jnp.bfloat16)
        state = jnp.zeros((HEAD, 2 * HEAD), jnp.float32)
        for c in range(0, positions, CHUNK):
            q, k = query[:, c : c + CHUNK], keys[:, c : c + CHUNK]
            wide = jnp.concatenate([v[c : c + CHUNK], ones], axis=1)
            a = jnp.where(causal, dot(q, k, ((0,), (0,))), 0.0).astype(jnp.bfloat16)
            both = dot(a, wide, ((1,), (0,)))
            if c:
                high = state.astype(jnp.bfloat16)
                low = (state - high.astype(jnp.float32)).astype(jnp.bfloat16)
                both = both + dot(q, high, ((0,), (0,))) + dot(q, low, ((0,), (0,)))
            out_ref[c : c + CHUNK, cols] = (both[:, :HEAD] / both[:, HEAD:]).astype(jnp.bfloat16)
            if c + CHUNK < positions:
                state = state + dot(k, wide, ((1,), (0,)))


def join_kernel(where_ref, y_ref, attn_ref, readout_ref, out_ref, sums_ref):
    start, length = where_ref[0] * y_ref.shape[0], where_ref[1]
    pieces, group, wide = attn_ref.shape
    row = start + lax.broadcasted_iota(jnp.int32, (group, 128), 0)
    valid = (row < length).astype(jnp.float32)
    last = (row == length - 1).astype(jnp.float32)
    product = jnp.zeros((group, 128), jnp.float32)
    squares = jnp.zeros((group, 128), jnp.float32)
    for j in range(pieces):
        for i in range(0, wide, 128):
            at = j * wide + i
            part = y_ref[:, at : at + 128].astype(jnp.float32)
            part = (part + attn_ref[j, :, i : i + 128].astype(jnp.float32)) * valid
            part = part.astype(jnp.bfloat16)
            out_ref[:, at : at + 128] = part
            part = part.astype(jnp.float32) * last
            product = product + part * readout_ref[:, at : at + 128].astype(jnp.float32)
            squares = squares + part * part
    product = jnp.sum(jnp.sum(product, axis=0, keepdims=True), axis=1, keepdims=True)
    squares = jnp.sum(jnp.sum(squares, axis=0, keepdims=True), axis=1, keepdims=True)
    lane = lax.broadcasted_iota(jnp.int32, sums_ref.shape, 1)
    sums_ref[...] = jnp.where(lane == 0, product, jnp.where(lane == 1, squares, 0.0))


def passed_along(block, axis, distance):
    devices = range(lax.axis_size(axis))
    route = [((i - distance) % len(devices), i) for i in devices]
    return lax.ppermute(block, axis, route)


def vmem():
    return pl.BlockSpec(memory_space=pltpu.VMEM)


def smem():
    return pl.BlockSpec(memory_space=pltpu.SMEM)


def body(
    pending_activity,
    entry_rescale_vector,
    probe_lifting_matrices,
    lookup_lifting_matrices,
    usable_extents,
    payoff_readout_vector,
):
    blocks = lax.axis_size("ctx")
    group, width = pending_activity.shape[2:]
    heads = probe_lifting_matrices.shape[2]
    mine = heads // blocks
    wide = mine * HEAD
    positions = blocks * group
    y = pending_activity[0, 0]
    where = jnp.stack([lax.axis_index("ctx").astype(jnp.int32), usable_extents[0, 0]])

    squares = pl.pallas_call(
        squares_kernel,
        out_shape=jax.ShapeDtypeStruct((1, group), jnp.float32),
        in_specs=[vmem()],
        out_specs=vmem(),
    )(y)
    squares = lax.psum(squares, "tp")
    normed = pl.pallas_call(
        norm_kernel,
        out_shape=jax.ShapeDtypeStruct((blocks, group, wide), jnp.bfloat16),
        in_specs=[vmem()] * 3,
        out_specs=vmem(),
    )(y, squares, entry_rescale_vector[0])
    values = lax.all_to_all(normed, "ctx", split_axis=0, concat_axis=0, tiled=True)

    weights = pl.BlockSpec((mine, HEAD, HEAD // 2), lambda g, w: (w[0], 0, 0))
    whole = pl.BlockSpec((positions, wide), lambda g, w: (0, 0))
    attn = pl.pallas_call(
        heads_kernel,
        out_shape=jax.ShapeDtypeStruct((positions, wide), jnp.bfloat16),
        grid_spec=pltpu.PrefetchScalarGridSpec(
            num_scalar_prefetch=1,
            grid=(1,),
            in_specs=[whole, weights, weights],
            out_specs=whole,
        ),
        compiler_params=pltpu.CompilerParams(vmem_limit_bytes=32 * 1024 * 1024),
    )(where, values.reshape(positions, wide), probe_lifting_matrices[0, 0], lookup_lifting_matrices[0, 0])
    attn = lax.all_to_all(
        attn.reshape(blocks, group, wide), "ctx", split_axis=0, concat_axis=0, tiled=True
    )

    out, sums = pl.pallas_call(
        join_kernel,
        out_shape=(
            jax.ShapeDtypeStruct((group, width), jnp.bfloat16),
            jax.ShapeDtypeStruct((blocks, 128), jnp.float32),
        ),
        in_specs=[smem(), vmem(), vmem(), vmem()],
        out_specs=(vmem(), vmem()),
    )(where, y, attn, payoff_readout_vector[None])
    handed = passed_along(out[None, None], "pipe", 1)
    sums = lax.psum(sums, "tp")
    sums = jnp.sum(lax.all_to_all(sums, "ctx", split_axis=0, concat_axis=0, tiled=True), axis=0)
    found = sums[0] * lax.rsqrt(sums[1] / EMBED_DIMENSION + eps_norm)
    return (handed, found[None, None])


def solution(mesh):
    placed = (
        P("pipe", None, "ctx", "tp"),
        P("pipe", None, "tp"),
        P("pipe", None, "tp", None, None),
        P("pipe", None, "tp", None, None),
        P("pipe", None),
        P("tp"),
    )
    return jax.shard_map(
        body,
        mesh=mesh,
        in_specs=placed,
        out_specs=(P("pipe", None, "ctx", "tp"), P("pipe", None)),
        check_vma=False,
    )
```

```python
import jax
import jax.numpy as jnp
from jax import lax
from jax.experimental import pallas as pl
from jax.experimental.pallas import tpu as pltpu
from jax.sharding import PartitionSpec as P

EMBED_DIMENSION = 8192
HEAD = 128
SPLIT = 4
EXTRA = 8

eps_norm = 1e-05


def three(value):
    parts = []
    for _ in range(3):
        parts.append(value.astype(jnp.bfloat16).astype(jnp.float32))
        value = value - parts[-1]
    return parts


def cut_kernel(y_ref, pieces_ref):
    blocks, group = pieces_ref.shape[0], y_ref.shape[0]
    heads = y_ref.shape[1] // HEAD // blocks
    total = jnp.zeros((group, HEAD), jnp.float32)
    for j in range(blocks):
        for h in range(heads):
            cols = slice((j * heads + h) * HEAD, (j * heads + h + 1) * HEAD)
            part = y_ref[:, cols]
            pieces_ref[j, h * group : (h + 1) * group, :] = part
            part = part.astype(jnp.float32)
            total = total + part * part
    total = jnp.concatenate([total, jnp.zeros((HEAD - group, HEAD), jnp.float32)], axis=0)
    total = jnp.sum(total.T, axis=0, keepdims=True)
    rows = three(total) + [jnp.zeros((EXTRA - 3, HEAD), jnp.float32)]
    rows = jnp.concatenate(rows, axis=0).astype(jnp.bfloat16)
    for j in range(blocks):
        pieces_ref[j, heads * group :, :] = rows


def feature(u):
    up = jnp.exp(u - jnp.max(u, axis=0, keepdims=True))
    down = jnp.exp(jnp.min(u, axis=0, keepdims=True) - u)
    up = up * (1.0 / jnp.sum(up, axis=0, keepdims=True))
    down = down * (1.0 / jnp.sum(down, axis=0, keepdims=True))
    return jnp.concatenate([up, down], axis=0)


def dot(a, b, dims):
    return lax.dot_general(a, b, (dims, ((), ())), preferred_element_type=jnp.float32)


def heads_kernel(
    where_ref, y_ref, squares_ref, gain_ref, probe_ref, lookup_ref, readout_ref, out_ref
):
    length = where_ref[1]
    blocks, heads = y_ref.shape[0], probe_ref.shape[0]
    group = (y_ref.shape[1] - EXTRA) // heads
    lines = blocks // SPLIT
    positions, chunk = blocks * group, SPLIT * group
    causal = lax.broadcasted_iota(jnp.int32, (chunk, chunk), 0) >= lax.broadcasted_iota(
        jnp.int32, (chunk, chunk), 1
    )
    at = lax.broadcasted_iota(jnp.int32, (chunk, HEAD), 0)
    valid = (lax.broadcasted_iota(jnp.int32, (1, positions), 1) < length).astype(jnp.float32)
    ones = jnp.ones((chunk, HEAD), jnp.bfloat16)
    scales = []
    for j in range(blocks):
        row = squares_ref[j : j + 1, :group]
        scale = lax.rsqrt(row / EMBED_DIMENSION + eps_norm)
        scales.append(jnp.broadcast_to(scale, (HEAD, group)).T)
    product = jnp.zeros((1, 1), jnp.float32)
    squares = jnp.zeros((1, 1), jnp.float32)
    for h in range(heads):
        rows = slice(h * group, (h + 1) * group)
        y = [y_ref[j, rows, :].astype(jnp.float32) for j in range(blocks)]
        gain = gain_ref[h].astype(jnp.float32)
        v = [(y[j] * scales[j] * gain).astype(jnp.bfloat16) for j in range(blocks)]
        v = jnp.concatenate(v, axis=0)
        query = feature(dot(probe_ref[h], v, ((0,), (1,)))).astype(jnp.bfloat16)
        keys = (feature(dot(lookup_ref[h], v, ((0,), (1,)))) * valid).astype(jnp.bfloat16)
        state = jnp.zeros((HEAD, 2 * HEAD), jnp.float32)
        last = jnp.zeros((1, HEAD), jnp.float32)
        for x in range(lines):
            cut = slice(x * chunk, (x + 1) * chunk)
            q, k = query[:, cut], keys[:, cut]
            wide = jnp.concatenate([v[cut], ones], axis=1)
            a = jnp.where(causal, dot(q, k, ((0,), (0,))), 0.0).astype(jnp.bfloat16)
            both = dot(a, wide, ((1,), (0,)))
            if x:
                high = state.astype(jnp.bfloat16)
                low = (state - high.astype(jnp.float32)).astype(jnp.bfloat16)
                both = both + dot(q, high, ((0,), (0,))) + dot(q, low, ((0,), (0,)))
            out = both[:, :HEAD] / both[:, HEAD:]
            out = out + jnp.concatenate(y[x * SPLIT : (x + 1) * SPLIT], axis=0)
            out = jnp.where(at < length - x * chunk, out, 0.0).astype(jnp.bfloat16)
            for z in range(SPLIT):
                out_ref[x * SPLIT + z, rows, :] = out[z * group : (z + 1) * group]
            out = jnp.where(at == length - 1 - x * chunk, out.astype(jnp.float32), 0.0)
            last = last + jnp.sum(out, axis=0, keepdims=True)
            if x + 1 < lines:
                state = state + dot(k, wide, ((1,), (0,)))
        product = product + jnp.sum(last * readout_ref[h].astype(jnp.float32), axis=1, keepdims=True)
        squares = squares + jnp.sum(last * last, axis=1, keepdims=True)
    lane = lax.broadcasted_iota(jnp.int32, (EXTRA, HEAD), 1)
    sums = jnp.zeros((EXTRA, HEAD), jnp.float32)
    for n, part in enumerate(three(product) + three(squares)):
        sums = jnp.where(lane == n, part, sums)
    for j in range(blocks):
        out_ref[j, heads * group :, :] = sums.astype(jnp.bfloat16)


def vmem():
    return pl.BlockSpec(memory_space=pltpu.VMEM)


def body(
    pending_activity,
    entry_rescale_vector,
    probe_lifting_matrices,
    lookup_lifting_matrices,
    usable_extents,
    payoff_readout_vector,
):
    blocks, sections = lax.axis_size("ctx"), lax.axis_size("pipe")
    group, width = pending_activity.shape[2:]
    y = pending_activity[0, 0]
    probe, lookup = probe_lifting_matrices[0, 0], lookup_lifting_matrices[0, 0]
    heads = probe.shape[0] // blocks
    readout = payoff_readout_vector.reshape(-1, 1, HEAD)
    gain = entry_rescale_vector.reshape(-1, 1, HEAD)
    where = jnp.stack([lax.axis_index("ctx").astype(jnp.int32), usable_extents[0, 0]])

    shape = (blocks, heads * group + EXTRA, HEAD)
    pieces = pl.pallas_call(
        cut_kernel,
        out_shape=jax.ShapeDtypeStruct(shape, jnp.bfloat16),
        in_specs=[vmem()],
        out_specs=vmem(),
    )(y)
    pieces = lax.all_to_all(pieces, "ctx", split_axis=0, concat_axis=0, tiled=True)
    squares = jnp.sum(pieces[:, heads * group : heads * group + 3, :].astype(jnp.float32), axis=1)
    squares = lax.psum(squares, "tp")

    def mine(*tail):
        return pl.BlockSpec((heads, *tail), lambda g, w: (w[0], *(0 for _ in tail)))

    def whole(*shape):
        return pl.BlockSpec(shape, lambda g, w: (0,) * len(shape))

    weights = mine(HEAD, HEAD // 2)
    out = pl.pallas_call(
        heads_kernel,
        out_shape=jax.ShapeDtypeStruct(shape, jnp.bfloat16),
        grid_spec=pltpu.PrefetchScalarGridSpec(
            num_scalar_prefetch=1,
            grid=(1,),
            in_specs=[
                whole(*shape),
                whole(*squares.shape),
                mine(1, HEAD),
                weights,
                weights,
                mine(1, HEAD),
            ],
            out_specs=whole(*shape),
        ),
        compiler_params=pltpu.CompilerParams(vmem_limit_bytes=32 * 1024 * 1024),
    )(where, pieces, squares, gain, probe, lookup, readout)
    out = lax.all_to_all(out, "ctx", split_axis=0, concat_axis=0, tiled=True)
    sums = jnp.sum(out[:, heads * group, :].astype(jnp.float32), axis=0)
    handed = lax.ppermute(out, "pipe", [(p, (p + 1) % sections) for p in range(sections)])
    handed = handed[:, : heads * group].reshape(blocks, heads, group, HEAD)
    handed = handed.transpose(2, 0, 1, 3).reshape(group, width)
    sums = lax.psum(sums, "tp")
    found = jnp.sum(sums[:3]) * lax.rsqrt(jnp.sum(sums[3:6]) / EMBED_DIMENSION + eps_norm)
    return (handed[None, None], found[None, None])


def solution(mesh):
    placed = (
        P("pipe", None, "ctx", "tp"),
        P("pipe", None, "tp"),
        P("pipe", None, "tp", None, None),
        P("pipe", None, "tp", None, None),
        P("pipe", None),
        P("tp"),
    )
    return jax.shard_map(
        body,
        mesh=mesh,
        in_specs=placed,
        out_specs=(P("pipe", None, "ctx", "tp"), P("pipe", None)),
        check_vma=False,
    )
```

```python
import jax
import jax.numpy as jnp
from jax import lax
from jax.experimental import pallas as pl
from jax.experimental.pallas import tpu as pltpu
from jax.sharding import PartitionSpec as P

EMBED_DIMENSION = 8192
HEAD = 128
SPLIT = 4
EXTRA = 8

eps_norm = 1e-05


def ordered(blocks):
    lines, far = blocks // SPLIT, SPLIT // 2
    return [x * SPLIT + z + far * n for z in range(far) for x in range(lines) for n in range(2)]


def three(value):
    parts = []
    for _ in range(3):
        parts.append(value.astype(jnp.bfloat16).astype(jnp.float32))
        value = value - parts[-1]
    return parts


def cut_kernel(y_ref, pieces_ref):
    blocks, group = pieces_ref.shape[0], y_ref.shape[0]
    heads = y_ref.shape[1] // HEAD // blocks
    total = jnp.zeros((group, HEAD), jnp.float32)
    for n, j in enumerate(ordered(blocks)):
        for h in range(heads):
            cols = slice((j * heads + h) * HEAD, (j * heads + h + 1) * HEAD)
            part = y_ref[:, cols]
            pieces_ref[n, h * group : (h + 1) * group, :] = part
            part = part.astype(jnp.float32)
            total = total + part * part
    total = jnp.concatenate([total, jnp.zeros((HEAD - group, HEAD), jnp.float32)], axis=0)
    total = jnp.sum(total.T, axis=0, keepdims=True)
    rows = three(total) + [jnp.zeros((EXTRA - 3, HEAD), jnp.float32)]
    rows = jnp.concatenate(rows, axis=0).astype(jnp.bfloat16)
    for j in range(blocks):
        pieces_ref[j, heads * group :, :] = rows


def feature(u):
    up = jnp.exp(u - jnp.max(u, axis=0, keepdims=True))
    down = jnp.exp(jnp.min(u, axis=0, keepdims=True) - u)
    up = up * (1.0 / jnp.sum(up, axis=0, keepdims=True))
    down = down * (1.0 / jnp.sum(down, axis=0, keepdims=True))
    return jnp.concatenate([up, down], axis=0)


def dot(a, b, dims):
    return lax.dot_general(a, b, (dims, ((), ())), preferred_element_type=jnp.float32)


def heads_kernel(
    length_ref, y_ref, squares_ref, gain_ref, lifting_ref, readout_ref, out_ref
):
    length = length_ref[0, 0]
    blocks, heads = y_ref.shape[0], lifting_ref.shape[0]
    group = (y_ref.shape[1] - EXTRA) // heads
    lines = blocks // SPLIT
    positions, chunk = blocks * group, SPLIT * group
    causal = lax.broadcasted_iota(jnp.int32, (chunk, chunk), 0) >= lax.broadcasted_iota(
        jnp.int32, (chunk, chunk), 1
    )
    at = lax.broadcasted_iota(jnp.int32, (chunk, HEAD), 0)
    valid = (lax.broadcasted_iota(jnp.int32, (1, positions), 1) < length).astype(jnp.float32)
    ones = jnp.ones((chunk, HEAD), jnp.bfloat16)
    order = ordered(blocks)
    place = [order.index(j) for j in range(blocks)]
    scales = []
    for j in range(blocks):
        row = squares_ref[place[j] : place[j] + 1, :group]
        scale = lax.rsqrt(row / EMBED_DIMENSION + eps_norm)
        scales.append(jnp.broadcast_to(scale, (HEAD, group)).T)
    product = jnp.zeros((1, 1), jnp.float32)
    squares = jnp.zeros((1, 1), jnp.float32)
    for h in range(heads):
        rows = slice(h * group, (h + 1) * group)
        y = [y_ref[place[j], rows, :].astype(jnp.float32) for j in range(blocks)]
        gain = gain_ref[h : h + 1, :].astype(jnp.float32)
        v = [(y[j] * scales[j] * gain).astype(jnp.bfloat16) for j in range(blocks)]
        v = jnp.concatenate(v, axis=0)
        u = dot(lifting_ref[h], v, ((1,), (1,)))
        query = feature(u[: HEAD // 2]).astype(jnp.bfloat16)
        keys = (feature(u[HEAD // 2 :]) * valid).astype(jnp.bfloat16)
        state = jnp.zeros((HEAD, 2 * HEAD), jnp.float32)
        last = jnp.zeros((1, HEAD), jnp.float32)
        for x in range(lines):
            cut = slice(x * chunk, (x + 1) * chunk)
            q, k = query[:, cut], keys[:, cut]
            wide = jnp.concatenate([v[cut], ones], axis=1)
            a = jnp.where(causal, dot(q, k, ((0,), (0,))), 0.0).astype(jnp.bfloat16)
            both = dot(a, wide, ((1,), (0,)))
            if x:
                high = state.astype(jnp.bfloat16)
                low = (state - high.astype(jnp.float32)).astype(jnp.bfloat16)
                both = both + dot(q, high, ((0,), (0,))) + dot(q, low, ((0,), (0,)))
            out = both[:, :HEAD] / both[:, HEAD:]
            out = out + jnp.concatenate(y[x * SPLIT : (x + 1) * SPLIT], axis=0)
            out = jnp.where(at < length - x * chunk, out, 0.0).astype(jnp.bfloat16)
            for z in range(SPLIT):
                out_ref[place[x * SPLIT + z], rows, :] = out[z * group : (z + 1) * group]
            out = jnp.where(at == length - 1 - x * chunk, out.astype(jnp.float32), 0.0)
            last = last + jnp.sum(out, axis=0, keepdims=True)
            if x + 1 < lines:
                state = state + dot(k, wide, ((1,), (0,)))
        product = product + jnp.sum(last * readout_ref[h : h + 1, :].astype(jnp.float32), axis=1, keepdims=True)
        squares = squares + jnp.sum(last * last, axis=1, keepdims=True)
    lane = lax.broadcasted_iota(jnp.int32, (EXTRA, HEAD), 1)
    sums = jnp.zeros((EXTRA, HEAD), jnp.float32)
    for n, part in enumerate(three(product) + three(squares)):
        sums = jnp.where(lane == n, part, sums)
    for j in range(blocks):
        out_ref[j, heads * group :, :] = sums.astype(jnp.bfloat16)


def exchanged(pieces):
    return lax.all_to_all(
        pieces,
        "ctx",
        split_axis=0,
        concat_axis=0,
        axis_index_groups=[ordered(lax.axis_size("ctx"))],
        tiled=True,
    )


def vmem():
    return pl.BlockSpec(memory_space=pltpu.VMEM)


def body(
    pending_activity,
    entry_rescale_vector,
    probe_lifting_matrices,
    lookup_lifting_matrices,
    usable_extents,
    payoff_readout_vector,
):
    blocks, sections = lax.axis_size("ctx"), lax.axis_size("pipe")
    group, width = pending_activity.shape[2:]
    y = pending_activity[0, 0]
    probe, lookup = probe_lifting_matrices[0, 0], lookup_lifting_matrices[0, 0]
    heads = probe.shape[0] // blocks
    first = lax.axis_index("ctx") * heads
    lifting = jnp.concatenate([probe.swapaxes(1, 2), lookup.swapaxes(1, 2)], axis=1)
    lifting = lax.dynamic_slice_in_dim(lifting, first, heads)
    gain = lax.dynamic_slice_in_dim(entry_rescale_vector.reshape(-1, HEAD), first, heads)
    readout = lax.dynamic_slice_in_dim(payoff_readout_vector.reshape(-1, HEAD), first, heads)

    shape = (blocks, heads * group + EXTRA, HEAD)
    pieces = pl.pallas_call(
        cut_kernel,
        out_shape=jax.ShapeDtypeStruct(shape, jnp.bfloat16),
        in_specs=[vmem()],
        out_specs=vmem(),
    )(y)
    pieces = exchanged(pieces)
    squares = jnp.sum(pieces[:, heads * group : heads * group + 3, :].astype(jnp.float32), axis=1)
    squares = lax.psum(squares, "tp")

    out = pl.pallas_call(
        heads_kernel,
        out_shape=jax.ShapeDtypeStruct(shape, jnp.bfloat16),
        in_specs=[pl.BlockSpec(memory_space=pltpu.SMEM)] + [vmem()] * 5,
        out_specs=vmem(),
        compiler_params=pltpu.CompilerParams(vmem_limit_bytes=32 * 1024 * 1024),
    )(usable_extents, pieces, squares, gain, lifting, readout)
    out = exchanged(out)
    sums = jnp.sum(out[:, heads * group, :].astype(jnp.float32), axis=0)
    handed = lax.ppermute(out, "pipe", [(p, (p + 1) % sections) for p in range(sections)])
    tiles = handed[:, : heads * group]
    tiles = tiles.reshape(SPLIT // 2, blocks // SPLIT, 2, heads, group // 8, 8, HEAD)
    tiles = tiles.transpose(4, 1, 2, 0, 3, 5, 6).reshape(group // 8, blocks * heads, 8, HEAD)
    tiles = lax.optimization_barrier(tiles)
    handed = tiles.transpose(0, 2, 1, 3).reshape(group, width)
    sums = lax.psum(sums, "tp")
    found = jnp.sum(sums[:3]) * lax.rsqrt(jnp.sum(sums[3:6]) / EMBED_DIMENSION + eps_norm)
    return (handed[None, None], found[None, None])


def solution(mesh):
    placed = (
        P("pipe", None, "ctx", "tp"),
        P("pipe", None, "tp"),
        P("pipe", None, "tp", None, None),
        P("pipe", None, "tp", None, None),
        P("pipe", None),
        P("tp"),
    )
    return jax.shard_map(
        body,
        mesh=mesh,
        in_specs=placed,
        out_specs=(P("pipe", None, "ctx", "tp"), P("pipe", None)),
        check_vma=False,
    )
```

```python
import jax
import jax.numpy as jnp
from jax import lax
from jax.experimental import pallas as pl
from jax.experimental.pallas import tpu as pltpu
from jax.sharding import PartitionSpec as P

EMBED_DIMENSION = 8192
HEAD = 128
SPLIT = 4
TURNS = (((0, 0), (0, 0)), ((0, 0), (0, 0)), ((0, 2), (1, 0)), ((0, 2), (1, 0)))
EXTRA = 8

eps_norm = 1e-05


def ordered(blocks):
    lines, far = blocks // SPLIT, SPLIT // 2
    return [x * SPLIT + z + far * n for z in range(far) for x in range(lines) for n in range(2)]


def three(value):
    parts = []
    for _ in range(3):
        parts.append(value.astype(jnp.bfloat16).astype(jnp.float32))
        value = value - parts[-1]
    return parts


def cut_kernel(y_ref, pieces_ref):
    blocks, group = pieces_ref.shape[0], y_ref.shape[0]
    heads = y_ref.shape[1] // HEAD // blocks
    total = jnp.zeros((group, HEAD), jnp.float32)
    for n, j in enumerate(ordered(blocks)):
        for h in range(heads):
            cols = slice((j * heads + h) * HEAD, (j * heads + h + 1) * HEAD)
            part = y_ref[:, cols]
            pieces_ref[n, h * group : (h + 1) * group, :] = part
            part = part.astype(jnp.float32)
            total = total + part * part
    total = jnp.concatenate([total, jnp.zeros((HEAD - group, HEAD), jnp.float32)], axis=0)
    total = jnp.sum(total.T, axis=0, keepdims=True)
    rows = three(total) + [jnp.zeros((EXTRA - 3, HEAD), jnp.float32)]
    rows = jnp.concatenate(rows, axis=0).astype(jnp.bfloat16)
    for j in range(blocks):
        pieces_ref[j, heads * group :, :] = rows


def feature(u):
    up = jnp.exp(u - jnp.max(u, axis=0, keepdims=True))
    down = jnp.exp(jnp.min(u, axis=0, keepdims=True) - u)
    up = up * (1.0 / jnp.sum(up, axis=0, keepdims=True))
    down = down * (1.0 / jnp.sum(down, axis=0, keepdims=True))
    return jnp.concatenate([up, down], axis=0)


def dot(a, b, dims):
    return lax.dot_general(a, b, (dims, ((), ())), preferred_element_type=jnp.float32)


def heads_kernel(
    length_ref, y_ref, squares_ref, gain_ref, lifting_ref, readout_ref, *refs
):
    out_ref = refs[-1]
    length = length_ref[0, 0]
    blocks, heads = y_ref.shape[0], lifting_ref.shape[0]
    group = (y_ref.shape[1] - EXTRA) // heads
    lines = blocks // SPLIT
    positions, chunk = blocks * group, SPLIT * group
    causal = lax.broadcasted_iota(jnp.int32, (chunk, chunk), 0) >= lax.broadcasted_iota(
        jnp.int32, (chunk, chunk), 1
    )
    at = lax.broadcasted_iota(jnp.int32, (chunk, HEAD), 0)
    valid = (lax.broadcasted_iota(jnp.int32, (1, positions), 1) < length).astype(jnp.float32)
    ones = jnp.ones((chunk, HEAD), jnp.bfloat16)
    order = ordered(blocks)
    place = [order.index(j) for j in range(blocks)]
    scales = []
    for j in range(blocks):
        row = squares_ref[place[j] : place[j] + 1, :group]
        scale = lax.rsqrt(row / EMBED_DIMENSION + eps_norm)
        scales.append(jnp.broadcast_to(scale, (HEAD, group)).T)
    product = jnp.zeros((1, 1), jnp.float32)
    squares = jnp.zeros((1, 1), jnp.float32)
    for h in range(heads):
        rows = slice(h * group, (h + 1) * group)
        y = [y_ref[place[j], rows, :].astype(jnp.float32) for j in range(blocks)]
        gain = gain_ref[h : h + 1, :].astype(jnp.float32)
        v = [(y[j] * scales[j] * gain).astype(jnp.bfloat16) for j in range(blocks)]
        v = jnp.concatenate(v, axis=0)
        u = dot(lifting_ref[h], v, ((1,), (1,)))
        query = feature(u[: HEAD // 2]).astype(jnp.bfloat16)
        keys = (feature(u[HEAD // 2 :]) * valid).astype(jnp.bfloat16)
        state = jnp.zeros((HEAD, 2 * HEAD), jnp.float32)
        last = jnp.zeros((1, HEAD), jnp.float32)
        for x in range(lines):
            cut = slice(x * chunk, (x + 1) * chunk)
            q, k = query[:, cut], keys[:, cut]
            wide = jnp.concatenate([v[cut], ones], axis=1)
            a = jnp.where(causal, dot(q, k, ((0,), (0,))), 0.0).astype(jnp.bfloat16)
            both = dot(a, wide, ((1,), (0,)))
            if x:
                high = state.astype(jnp.bfloat16)
                low = (state - high.astype(jnp.float32)).astype(jnp.bfloat16)
                both = both + dot(q, high, ((0,), (0,))) + dot(q, low, ((0,), (0,)))
            out = both[:, :HEAD] / both[:, HEAD:]
            out = out + jnp.concatenate(y[x * SPLIT : (x + 1) * SPLIT], axis=0)
            out = jnp.where(at < length - x * chunk, out, 0.0).astype(jnp.bfloat16)
            for z in range(SPLIT):
                out_ref[place[x * SPLIT + z], rows, :] = out[z * group : (z + 1) * group]
            out = jnp.where(at == length - 1 - x * chunk, out.astype(jnp.float32), 0.0)
            last = last + jnp.sum(out, axis=0, keepdims=True)
            if x + 1 < lines:
                state = state + dot(k, wide, ((1,), (0,)))
        product = product + jnp.sum(last * readout_ref[h : h + 1, :].astype(jnp.float32), axis=1, keepdims=True)
        squares = squares + jnp.sum(last * last, axis=1, keepdims=True)
    lane = lax.broadcasted_iota(jnp.int32, (EXTRA, HEAD), 1)
    sums = jnp.zeros((EXTRA, HEAD), jnp.float32)
    for n, part in enumerate(three(product) + three(squares)):
        sums = jnp.where(lane == n, part, sums)
    for j in range(blocks):
        out_ref[j, heads * group :, :] = sums.astype(jnp.bfloat16)


def exchanged(pieces):
    return lax.all_to_all(
        pieces,
        "ctx",
        split_axis=0,
        concat_axis=0,
        axis_index_groups=[ordered(lax.axis_size("ctx"))],
        tiled=True,
    )


def vmem():
    return pl.BlockSpec(memory_space=pltpu.VMEM)


def body(
    pending_activity,
    entry_rescale_vector,
    probe_lifting_matrices,
    lookup_lifting_matrices,
    usable_extents,
    payoff_readout_vector,
):
    blocks, sections = lax.axis_size("ctx"), lax.axis_size("pipe")
    group, width = pending_activity.shape[2:]
    y = pending_activity[0, 0]
    probe, lookup = probe_lifting_matrices[0, 0], lookup_lifting_matrices[0, 0]
    heads = probe.shape[0] // blocks
    first = lax.axis_index("ctx") * heads
    lifting = jnp.concatenate([probe.swapaxes(1, 2), lookup.swapaxes(1, 2)], axis=1)
    lifting = lax.dynamic_slice_in_dim(lifting, first, heads)
    gain = lax.dynamic_slice_in_dim(entry_rescale_vector.reshape(-1, HEAD), first, heads)
    readout = lax.dynamic_slice_in_dim(payoff_readout_vector.reshape(-1, HEAD), first, heads)

    shape = (blocks, heads * group + EXTRA, HEAD)
    pieces = pl.pallas_call(
        cut_kernel,
        out_shape=jax.ShapeDtypeStruct(shape, jnp.bfloat16),
        in_specs=[vmem()],
        out_specs=vmem(),
    )(y)
    lines, size = blocks // SPLIT, sections // len(TURNS)
    turn, turns = usable_extents, []
    for heard in zip(*TURNS):
        route = [
            (p * blocks + x * SPLIT + z, p * blocks + (x + dx) % lines * SPLIT + (z + dz) % SPLIT)
            for p in range(sections)
            for x in range(lines)
            for z in range(SPLIT)
            for dx, dz in [heard[p // size]]
            if dx or dz
        ]
        turn = lax.ppermute(turn, ("pipe", "ctx"), route)
        turns.append(turn)
    pieces, *turns = lax.optimization_barrier((pieces, *turns))
    pieces = exchanged(pieces)
    squares = jnp.sum(pieces[:, heads * group : heads * group + 3, :].astype(jnp.float32), axis=1)
    squares = lax.psum(squares, "tp")

    out = pl.pallas_call(
        heads_kernel,
        out_shape=jax.ShapeDtypeStruct(shape, jnp.bfloat16),
        in_specs=[pl.BlockSpec(memory_space=pltpu.SMEM)]
        + [vmem()] * 5
        + [pl.BlockSpec(memory_space=pl.ANY)] * len(turns),
        out_specs=vmem(),
        compiler_params=pltpu.CompilerParams(vmem_limit_bytes=32 * 1024 * 1024),
    )(usable_extents, pieces, squares, gain, lifting, readout, *turns)
    out = exchanged(out)
    sums = jnp.sum(out[:, heads * group, :].astype(jnp.float32), axis=0)
    handed = lax.ppermute(out, "pipe", [(p, (p + 1) % sections) for p in range(sections)])
    tiles = handed[:, : heads * group]
    tiles = tiles.reshape(SPLIT // 2, blocks // SPLIT, 2, heads, group // 8, 8, HEAD)
    tiles = tiles.transpose(4, 1, 2, 0, 3, 5, 6).reshape(group // 8, blocks * heads, 8, HEAD)
    tiles = lax.optimization_barrier(tiles)
    handed = tiles.transpose(0, 2, 1, 3).reshape(group, width)
    sums = lax.psum(sums, "tp")
    found = jnp.sum(sums[:3]) * lax.rsqrt(jnp.sum(sums[3:6]) / EMBED_DIMENSION + eps_norm)
    return (handed[None, None], found[None, None])


def solution(mesh):
    placed = (
        P("pipe", None, "ctx", "tp"),
        P("pipe", None, "tp"),
        P("pipe", None, "tp", None, None),
        P("pipe", None, "tp", None, None),
        P("pipe", None),
        P("tp"),
    )
    return jax.shard_map(
        body,
        mesh=mesh,
        in_specs=placed,
        out_specs=(P("pipe", None, "ctx", "tp"), P("pipe", None)),
        check_vma=False,
    )
```

```python
import jax
import jax.numpy as jnp
from jax import lax
from jax.experimental import pallas as pl
from jax.experimental.pallas import tpu as pltpu
from jax.sharding import PartitionSpec as P

EMBED_DIMENSION = 8192
HEAD = 128
SPLIT = 4
TURNS = ((2, 2, 2),)
EXTRA = 8

eps_norm = 1e-05


def ordered(blocks):
    lines, far = blocks // SPLIT, SPLIT // 2
    return [x * SPLIT + z + far * n for z in range(far) for x in range(lines) for n in range(2)]


def three(value):
    parts = []
    for _ in range(3):
        parts.append(value.astype(jnp.bfloat16).astype(jnp.float32))
        value = value - parts[-1]
    return parts


def squares_kernel(y_ref, out_ref):
    total = jnp.zeros((y_ref.shape[0], HEAD), jnp.float32)
    for j in range(0, y_ref.shape[1], HEAD):
        part = y_ref[:, j : j + HEAD].astype(jnp.float32)
        total = total + part * part
    out_ref[...] = jnp.sum(total.T, axis=0, keepdims=True)


def cut_kernel(y_ref, squares_ref, pieces_ref):
    blocks, group = pieces_ref.shape[0], y_ref.shape[0]
    heads = y_ref.shape[1] // HEAD // blocks
    for n, j in enumerate(ordered(blocks)):
        for h in range(heads):
            cols = slice((j * heads + h) * HEAD, (j * heads + h + 1) * HEAD)
            pieces_ref[n, h * group : (h + 1) * group, :] = y_ref[:, cols]
    total = jnp.concatenate([squares_ref[...], jnp.zeros((1, HEAD - group), jnp.float32)], axis=1)
    rows = three(total) + [jnp.zeros((EXTRA - 3, HEAD), jnp.float32)]
    rows = jnp.concatenate(rows, axis=0).astype(jnp.bfloat16)
    for j in range(blocks):
        pieces_ref[j, heads * group :, :] = rows


def feature(u):
    up = jnp.exp(u - jnp.max(u, axis=0, keepdims=True))
    down = jnp.exp(jnp.min(u, axis=0, keepdims=True) - u)
    up = up * (1.0 / jnp.sum(up, axis=0, keepdims=True))
    down = down * (1.0 / jnp.sum(down, axis=0, keepdims=True))
    return jnp.concatenate([up, down], axis=0)


def dot(a, b, dims):
    return lax.dot_general(a, b, (dims, ((), ())), preferred_element_type=jnp.float32)


def heads_kernel(
    length_ref, y_ref, gain_ref, lifting_ref, readout_ref, *refs
):
    out_ref = refs[-1]
    length, behind = length_ref[0, 0], length_ref[0, 1]
    blocks, heads = y_ref.shape[0], lifting_ref.shape[0]
    group = (y_ref.shape[1] - EXTRA) // heads
    lines = blocks // SPLIT
    positions, chunk = blocks * group, SPLIT * group
    causal = lax.broadcasted_iota(jnp.int32, (chunk, chunk), 0) >= lax.broadcasted_iota(
        jnp.int32, (chunk, chunk), 1
    )
    at = lax.broadcasted_iota(jnp.int32, (chunk, HEAD), 0)
    valid = (lax.broadcasted_iota(jnp.int32, (1, positions), 1) < length).astype(jnp.float32)
    ones = jnp.ones((chunk, HEAD), jnp.bfloat16)
    order = ordered(blocks)
    place = [order.index(j) for j in range(blocks)]
    scales = []
    for j in range(blocks):
        row = y_ref[place[j], heads * group :, :].astype(jnp.float32)
        row = jnp.sum(row, axis=0, keepdims=True)[:, :group]
        scale = lax.rsqrt(row / EMBED_DIMENSION + eps_norm)
        scales.append(jnp.broadcast_to(scale, (HEAD, group)).T)
    product = jnp.zeros((1, 1), jnp.float32)
    squares = jnp.zeros((1, 1), jnp.float32)
    for h in range(heads):
        rows = slice(h * group, (h + 1) * group)
        y = [y_ref[place[j], rows, :].astype(jnp.float32) for j in range(blocks)]
        gain = gain_ref[h : h + 1, :].astype(jnp.float32)
        v = [(y[j] * scales[j] * gain).astype(jnp.bfloat16) for j in range(blocks)]
        v = jnp.concatenate(v, axis=0)
        u = dot(lifting_ref[h], v, ((1,), (1,)))
        query = feature(u[: HEAD // 2]).astype(jnp.bfloat16)
        keys = (feature(u[HEAD // 2 :]) * valid).astype(jnp.bfloat16)
        state = jnp.zeros((HEAD, 2 * HEAD), jnp.float32)
        last = jnp.zeros((1, HEAD), jnp.float32)
        for x in range(lines):
            cut = slice(x * chunk, (x + 1) * chunk)
            q, k = query[:, cut], keys[:, cut]
            wide = jnp.concatenate([v[cut], ones], axis=1)
            a = jnp.where(causal, dot(q, k, ((0,), (0,))), 0.0).astype(jnp.bfloat16)
            both = dot(a, wide, ((1,), (0,)))
            if x:
                high = state.astype(jnp.bfloat16)
                low = (state - high.astype(jnp.float32)).astype(jnp.bfloat16)
                both = both + dot(q, high, ((0,), (0,))) + dot(q, low, ((0,), (0,)))
            out = both[:, :HEAD] / both[:, HEAD:]
            out = out + jnp.concatenate(y[x * SPLIT : (x + 1) * SPLIT], axis=0)
            out = jnp.where(at < length - x * chunk, out, 0.0).astype(jnp.bfloat16)
            for z in range(SPLIT):
                to = lax.rem(z + SPLIT - behind, SPLIT)
                to = lax.rem(to, SPLIT // 2) * 2 * lines + x * 2 + lax.div(to, SPLIT // 2)
                out_ref[to, rows, :] = out[z * group : (z + 1) * group]
            out = jnp.where(at == length - 1 - x * chunk, out.astype(jnp.float32), 0.0)
            last = last + jnp.sum(out, axis=0, keepdims=True)
            if x + 1 < lines:
                state = state + dot(k, wide, ((1,), (0,)))
        product = product + jnp.sum(last * readout_ref[h : h + 1, :].astype(jnp.float32), axis=1, keepdims=True)
        squares = squares + jnp.sum(last * last, axis=1, keepdims=True)
    lane = lax.broadcasted_iota(jnp.int32, (EXTRA, HEAD), 1)
    sums = jnp.zeros((EXTRA, HEAD), jnp.float32)
    for n, part in enumerate(three(product) + three(squares)):
        sums = jnp.where(lane == n, part, sums)
    for j in range(blocks):
        out_ref[j, heads * group :, :] = sums.astype(jnp.bfloat16)


def exchanged(pieces):
    return lax.all_to_all(
        pieces,
        "ctx",
        split_axis=0,
        concat_axis=0,
        axis_index_groups=[ordered(lax.axis_size("ctx"))],
        tiled=True,
    )


def vmem():
    return pl.BlockSpec(memory_space=pltpu.VMEM)


def body(
    pending_activity,
    entry_rescale_vector,
    probe_lifting_matrices,
    lookup_lifting_matrices,
    usable_extents,
    payoff_readout_vector,
):
    blocks, sections = lax.axis_size("ctx"), lax.axis_size("pipe")
    group, width = pending_activity.shape[2:]
    y = pending_activity[0, 0]
    probe, lookup = probe_lifting_matrices[0, 0], lookup_lifting_matrices[0, 0]
    heads = probe.shape[0] // blocks
    first = lax.axis_index("ctx") * heads
    lifting = jnp.concatenate([probe.swapaxes(1, 2), lookup.swapaxes(1, 2)], axis=1)
    lifting = lax.dynamic_slice_in_dim(lifting, first, heads)
    gain = lax.dynamic_slice_in_dim(entry_rescale_vector.reshape(-1, HEAD), first, heads)
    readout = lax.dynamic_slice_in_dim(payoff_readout_vector.reshape(-1, HEAD), first, heads)

    squares = pl.pallas_call(
        squares_kernel,
        out_shape=jax.ShapeDtypeStruct((1, group), jnp.float32),
        in_specs=[vmem()],
        out_specs=vmem(),
    )(y)
    squares = lax.psum(squares, "tp")
    turn, squares = lax.optimization_barrier((usable_extents, squares))
    lines, runs, sides, turns = blocks // SPLIT, 4, lax.axis_size("tp"), []
    for dy, dx, dz in TURNS:
        route = [
            (
                ((p * lines + x) * SPLIT + z) * sides + sides - 1,
                (
                    ((p // runs * runs + (p + dy) % runs) * lines + (x + dx) % lines) * SPLIT
                    + (z + dz) % SPLIT
                )
                * sides
                + sides
                - 1,
            )
            for p in range(sections)
            for x in range(lines)
            for z in range(SPLIT)
        ]
        turn = lax.ppermute(turn, ("pipe", "ctx", "tp"), route)
        turns.append(turn)

    shape = (blocks, heads * group + EXTRA, HEAD)
    pieces = pl.pallas_call(
        cut_kernel,
        out_shape=jax.ShapeDtypeStruct(shape, jnp.bfloat16),
        in_specs=[vmem(), vmem()],
        out_specs=vmem(),
    )(y, squares)
    pieces, *turns = lax.optimization_barrier((pieces, *turns))
    pieces = exchanged(pieces)
    behind = (lax.axis_index("pipe") == sections - 1).astype(jnp.int32)
    extents = jnp.concatenate([usable_extents, behind.reshape(1, 1)], axis=1)
    out = pl.pallas_call(
        heads_kernel,
        out_shape=jax.ShapeDtypeStruct(shape, jnp.bfloat16),
        in_specs=[pl.BlockSpec(memory_space=pltpu.SMEM)]
        + [vmem()] * 4
        + [pl.BlockSpec(memory_space=pl.ANY)] * len(turns),
        out_specs=vmem(),
        compiler_params=pltpu.CompilerParams(vmem_limit_bytes=32 * 1024 * 1024),
    )(extents, pieces, gain, lifting, readout, *turns)
    out = exchanged(out)
    sums = jnp.sum(out[:, heads * group, :].astype(jnp.float32), axis=0)
    route = [
        (
            (p * lines + x) * SPLIT + z,
            ((p + 1) % sections * lines + x) * SPLIT + (z + (p + 1) // sections) % SPLIT,
        )
        for p in range(sections)
        for x in range(lines)
        for z in range(SPLIT)
    ]
    handed = lax.ppermute(out, ("pipe", "ctx"), route)
    tiles = handed[:, : heads * group]
    tiles = tiles.reshape(SPLIT // 2, blocks // SPLIT, 2, heads, group // 8, 8, HEAD)
    tiles = tiles.transpose(4, 1, 2, 0, 3, 5, 6).reshape(group // 8, blocks * heads, 8, HEAD)
    tiles = lax.optimization_barrier(tiles)
    handed = tiles.transpose(0, 2, 1, 3).reshape(group, width)
    sums = lax.psum(sums, "tp")
    found = jnp.sum(sums[:3]) * lax.rsqrt(jnp.sum(sums[3:6]) / EMBED_DIMENSION + eps_norm)
    return (handed[None, None], found[None, None])


def solution(mesh):
    placed = (
        P("pipe", None, "ctx", "tp"),
        P("pipe", None, "tp"),
        P("pipe", None, "tp", None, None),
        P("pipe", None, "tp", None, None),
        P("pipe", None),
        P("tp"),
    )
    return jax.shard_map(
        body,
        mesh=mesh,
        in_specs=placed,
        out_specs=(P("pipe", None, "ctx", "tp"), P("pipe", None)),
        check_vma=False,
    )
```

```python
import jax
import jax.numpy as jnp
from jax import lax
from jax.experimental import pallas as pl
from jax.experimental.pallas import tpu as pltpu
from jax.sharding import PartitionSpec as P

EMBED_DIMENSION = 8192
HEAD = 128
SPLIT = 4
TURNS = ((2, 2, 2),)
EXTRA = 8

eps_norm = 1e-05


def ordered(blocks):
    lines, far = blocks // SPLIT, SPLIT // 2
    return [x * SPLIT + z + far * n for z in range(far) for x in range(lines) for n in range(2)]


def three(value):
    parts = []
    for _ in range(3):
        parts.append(value.astype(jnp.bfloat16).astype(jnp.float32))
        value = value - parts[-1]
    return parts


def squares_kernel(y_ref, out_ref):
    total = jnp.zeros((y_ref.shape[0], HEAD), jnp.float32)
    for j in range(0, y_ref.shape[1], HEAD):
        part = y_ref[:, j : j + HEAD].astype(jnp.float32)
        total = total + part * part
    out_ref[...] = jnp.sum(total.T, axis=0, keepdims=True)


def cut_kernel(y_ref, squares_ref, pieces_ref):
    blocks, group = pieces_ref.shape[0], y_ref.shape[0]
    heads = y_ref.shape[1] // HEAD // blocks
    for n, j in enumerate(ordered(blocks)):
        for h in range(heads):
            cols = slice((j * heads + h) * HEAD, (j * heads + h + 1) * HEAD)
            pieces_ref[n, h * group : (h + 1) * group, :] = y_ref[:, cols]
    total = jnp.concatenate([squares_ref[...], jnp.zeros((1, HEAD - group), jnp.float32)], axis=1)
    rows = three(total) + [jnp.zeros((EXTRA - 3, HEAD), jnp.float32)]
    rows = jnp.concatenate(rows, axis=0).astype(jnp.bfloat16)
    for j in range(blocks):
        pieces_ref[j, heads * group :, :] = rows


def feature(u):
    up = jnp.exp(u - jnp.max(u, axis=0, keepdims=True))
    down = jnp.exp(jnp.min(u, axis=0, keepdims=True) - u)
    up = up * (1.0 / jnp.sum(up, axis=0, keepdims=True))
    down = down * (1.0 / jnp.sum(down, axis=0, keepdims=True))
    return jnp.concatenate([up, down], axis=0)


def dot(a, b, dims):
    return lax.dot_general(a, b, (dims, ((), ())), preferred_element_type=jnp.float32)


def heads_kernel(
    length_ref, behind_ref, y_ref, squares_ref, gain_ref, lifting_ref, readout_ref, *refs
):
    out_ref = refs[-1]
    length, behind = length_ref[0, 0], behind_ref[0, 0]
    blocks, heads = y_ref.shape[0], lifting_ref.shape[0]
    group = (y_ref.shape[1] - EXTRA) // heads
    lines = blocks // SPLIT
    positions, chunk = blocks * group, SPLIT * group
    causal = lax.broadcasted_iota(jnp.int32, (chunk, chunk), 0) >= lax.broadcasted_iota(
        jnp.int32, (chunk, chunk), 1
    )
    at = lax.broadcasted_iota(jnp.int32, (chunk, HEAD), 0)
    valid = (lax.broadcasted_iota(jnp.int32, (1, positions), 1) < length).astype(jnp.float32)
    ones = jnp.ones((chunk, HEAD), jnp.bfloat16)
    order = ordered(blocks)
    place = [order.index(j) for j in range(blocks)]
    to = [lax.rem(z + SPLIT - behind, SPLIT) for z in range(SPLIT)]
    to = [lax.rem(z, SPLIT // 2) * 2 * lines + lax.div(z, SPLIT // 2) for z in to]
    scales = []
    for j in range(blocks):
        row = squares_ref[place[j] : place[j] + 1, :group]
        scale = lax.rsqrt(row / EMBED_DIMENSION + eps_norm)
        scales.append(jnp.broadcast_to(scale, (HEAD, group)).T)
    product = jnp.zeros((1, 1), jnp.float32)
    squares = jnp.zeros((1, 1), jnp.float32)
    for h in range(heads):
        rows = slice(h * group, (h + 1) * group)
        y = [y_ref[place[j], rows, :].astype(jnp.float32) for j in range(blocks)]
        gain = gain_ref[h : h + 1, :].astype(jnp.float32)
        v = [(y[j] * scales[j] * gain).astype(jnp.bfloat16) for j in range(blocks)]
        v = jnp.concatenate(v, axis=0)
        u = dot(lifting_ref[h], v, ((1,), (1,)))
        query = feature(u[: HEAD // 2]).astype(jnp.bfloat16)
        keys = (feature(u[HEAD // 2 :]) * valid).astype(jnp.bfloat16)
        state = jnp.zeros((HEAD, 2 * HEAD), jnp.float32)
        last = jnp.zeros((1, HEAD), jnp.float32)
        for x in range(lines):
            cut = slice(x * chunk, (x + 1) * chunk)
            q, k = query[:, cut], keys[:, cut]
            wide = jnp.concatenate([v[cut], ones], axis=1)
            a = jnp.where(causal, dot(q, k, ((0,), (0,))), 0.0).astype(jnp.bfloat16)
            both = dot(a, wide, ((1,), (0,)))
            if x:
                high = state.astype(jnp.bfloat16)
                low = (state - high.astype(jnp.float32)).astype(jnp.bfloat16)
                both = both + dot(q, high, ((0,), (0,))) + dot(q, low, ((0,), (0,)))
            out = both[:, :HEAD] / both[:, HEAD:]
            out = out + jnp.concatenate(y[x * SPLIT : (x + 1) * SPLIT], axis=0)
            out = jnp.where(at < length - x * chunk, out, 0.0).astype(jnp.bfloat16)
            for z in range(SPLIT):
                out_ref[to[z] + x * 2, rows, :] = out[z * group : (z + 1) * group]
            out = jnp.where(at == length - 1 - x * chunk, out.astype(jnp.float32), 0.0)
            last = last + jnp.sum(out, axis=0, keepdims=True)
            if x + 1 < lines:
                state = state + dot(k, wide, ((1,), (0,)))
        product = product + jnp.sum(last * readout_ref[h : h + 1, :].astype(jnp.float32), axis=1, keepdims=True)
        squares = squares + jnp.sum(last * last, axis=1, keepdims=True)
    lane = lax.broadcasted_iota(jnp.int32, (EXTRA, HEAD), 1)
    sums = jnp.zeros((EXTRA, HEAD), jnp.float32)
    for n, part in enumerate(three(product) + three(squares)):
        sums = jnp.where(lane == n, part, sums)
    for j in range(blocks):
        out_ref[j, heads * group :, :] = sums.astype(jnp.bfloat16)


def exchanged(pieces):
    return lax.all_to_all(
        pieces,
        "ctx",
        split_axis=0,
        concat_axis=0,
        axis_index_groups=[ordered(lax.axis_size("ctx"))],
        tiled=True,
    )


def vmem():
    return pl.BlockSpec(memory_space=pltpu.VMEM)


def body(
    pending_activity,
    entry_rescale_vector,
    probe_lifting_matrices,
    lookup_lifting_matrices,
    usable_extents,
    payoff_readout_vector,
):
    blocks, sections = lax.axis_size("ctx"), lax.axis_size("pipe")
    group, width = pending_activity.shape[2:]
    y = pending_activity[0, 0]
    probe, lookup = probe_lifting_matrices[0, 0], lookup_lifting_matrices[0, 0]
    heads = probe.shape[0] // blocks
    first = lax.axis_index("ctx") * heads
    lifting = jnp.concatenate([probe.swapaxes(1, 2), lookup.swapaxes(1, 2)], axis=1)
    lifting = lax.dynamic_slice_in_dim(lifting, first, heads)
    gain = lax.dynamic_slice_in_dim(entry_rescale_vector.reshape(-1, HEAD), first, heads)
    readout = lax.dynamic_slice_in_dim(payoff_readout_vector.reshape(-1, HEAD), first, heads)

    squares = pl.pallas_call(
        squares_kernel,
        out_shape=jax.ShapeDtypeStruct((1, group), jnp.float32),
        in_specs=[vmem()],
        out_specs=vmem(),
    )(y)
    squares = lax.psum(squares, "tp")
    turn = squares
    lines, runs, sides, turns = blocks // SPLIT, 4, lax.axis_size("tp"), []
    for dy, dx, dz in TURNS:
        route = [
            (
                ((p * lines + x) * SPLIT + z) * sides + sides - 1,
                (
                    ((p // runs * runs + (p + dy) % runs) * lines + (x + dx) % lines) * SPLIT
                    + (z + dz) % SPLIT
                )
                * sides
                + sides
                - 1,
            )
            for p in range(sections)
            for x in range(lines)
            for z in range(SPLIT)
        ]
        turn = lax.ppermute(turn, ("pipe", "ctx", "tp"), route)
        turns.append(turn)

    shape = (blocks, heads * group + EXTRA, HEAD)
    pieces = pl.pallas_call(
        cut_kernel,
        out_shape=jax.ShapeDtypeStruct(shape, jnp.bfloat16),
        in_specs=[vmem(), vmem()],
        out_specs=vmem(),
    )(y, squares)
    pieces, *turns = lax.optimization_barrier((pieces, *turns))
    pieces = exchanged(pieces)
    squares = jnp.sum(pieces[:, heads * group : heads * group + 3, :].astype(jnp.float32), axis=1)
    behind = (lax.axis_index("pipe") == sections - 1).astype(jnp.int32)
    out = pl.pallas_call(
        heads_kernel,
        out_shape=jax.ShapeDtypeStruct(shape, jnp.bfloat16),
        in_specs=[pl.BlockSpec(memory_space=pltpu.SMEM)] * 2
        + [vmem()] * 5
        + [pl.BlockSpec(memory_space=pl.ANY)] * len(turns),
        out_specs=vmem(),
        compiler_params=pltpu.CompilerParams(vmem_limit_bytes=32 * 1024 * 1024),
    )(usable_extents, behind.reshape(1, 1), pieces, squares, gain, lifting, readout, *turns)
    out = exchanged(out)
    sums = jnp.sum(out[:, heads * group, :].astype(jnp.float32), axis=0)
    route = [
        (
            (p * lines + x) * SPLIT + z,
            ((p + 1) % sections * lines + x) * SPLIT + (z + (p + 1) // sections) % SPLIT,
        )
        for p in range(sections)
        for x in range(lines)
        for z in range(SPLIT)
    ]
    handed = lax.ppermute(out, ("pipe", "ctx"), route)
    tiles = handed[:, : heads * group]
    tiles = tiles.reshape(SPLIT // 2, blocks // SPLIT, 2, heads, group // 8, 8, HEAD)
    tiles = tiles.transpose(4, 1, 2, 0, 3, 5, 6).reshape(group // 8, blocks * heads, 8, HEAD)
    tiles = lax.optimization_barrier(tiles)
    handed = tiles.transpose(0, 2, 1, 3).reshape(group, width)
    sums = lax.psum(sums, "tp")
    found = jnp.sum(sums[:3]) * lax.rsqrt(jnp.sum(sums[3:6]) / EMBED_DIMENSION + eps_norm)
    return (handed[None, None], found[None, None])


def solution(mesh):
    placed = (
        P("pipe", None, "ctx", "tp"),
        P("pipe", None, "tp"),
        P("pipe", None, "tp", None, None),
        P("pipe", None, "tp", None, None),
        P("pipe", None),
        P("tp"),
    )
    return jax.shard_map(
        body,
        mesh=mesh,
        in_specs=placed,
        out_specs=(P("pipe", None, "ctx", "tp"), P("pipe", None)),
        check_vma=False,
    )
```

```python
import jax
import jax.numpy as jnp
from jax import lax
from jax.experimental import pallas as pl
from jax.experimental.pallas import tpu as pltpu
from jax.sharding import PartitionSpec as P

EMBED_DIMENSION = 8192
HEAD = 128
SPLIT = 4
TURNS = ((2, 2, 2),)
EXTRA = 8

eps_norm = 1e-05


def ordered(blocks):
    lines, far = blocks // SPLIT, SPLIT // 2
    return [x * SPLIT + z + far * n for z in range(far) for x in range(lines) for n in range(2)]


def rotated(blocks):
    lines = blocks // SPLIT
    return [x * SPLIT + (z + x) % SPLIT for x in range(lines) for z in range(SPLIT)]


def three(value):
    parts = []
    for _ in range(3):
        parts.append(value.astype(jnp.bfloat16).astype(jnp.float32))
        value = value - parts[-1]
    return parts


def squares_kernel(y_ref, out_ref):
    total = jnp.zeros((y_ref.shape[0], HEAD), jnp.float32)
    for j in range(0, y_ref.shape[1], HEAD):
        part = y_ref[:, j : j + HEAD].astype(jnp.float32)
        total = total + part * part
    out_ref[...] = jnp.sum(total.T, axis=0, keepdims=True)


def cut_kernel(y_ref, squares_ref, pieces_ref):
    blocks, group = pieces_ref.shape[0], y_ref.shape[0]
    heads = y_ref.shape[1] // HEAD // blocks
    for n, j in enumerate(rotated(blocks)):
        for h in range(heads):
            cols = slice((j * heads + h) * HEAD, (j * heads + h + 1) * HEAD)
            pieces_ref[n, h * group : (h + 1) * group, :] = y_ref[:, cols]
    total = jnp.concatenate([squares_ref[...], jnp.zeros((1, HEAD - group), jnp.float32)], axis=1)
    rows = three(total) + [jnp.zeros((EXTRA - 3, HEAD), jnp.float32)]
    rows = jnp.concatenate(rows, axis=0).astype(jnp.bfloat16)
    for j in range(blocks):
        pieces_ref[j, heads * group :, :] = rows


def feature(u):
    up = jnp.exp(u - jnp.max(u, axis=0, keepdims=True))
    down = jnp.exp(jnp.min(u, axis=0, keepdims=True) - u)
    up = up * (1.0 / jnp.sum(up, axis=0, keepdims=True))
    down = down * (1.0 / jnp.sum(down, axis=0, keepdims=True))
    return jnp.concatenate([up, down], axis=0)


def dot(a, b, dims):
    return lax.dot_general(a, b, (dims, ((), ())), preferred_element_type=jnp.float32)


def heads_kernel(
    length_ref, behind_ref, y_ref, squares_ref, gain_ref, lifting_ref, readout_ref, *refs
):
    out_ref = refs[-1]
    length, behind = length_ref[0, 0], behind_ref[0, 0]
    blocks, heads = y_ref.shape[0], lifting_ref.shape[0]
    group = (y_ref.shape[1] - EXTRA) // heads
    lines = blocks // SPLIT
    positions, chunk = blocks * group, SPLIT * group
    causal = lax.broadcasted_iota(jnp.int32, (chunk, chunk), 0) >= lax.broadcasted_iota(
        jnp.int32, (chunk, chunk), 1
    )
    at = lax.broadcasted_iota(jnp.int32, (chunk, HEAD), 0)
    valid = (lax.broadcasted_iota(jnp.int32, (1, positions), 1) < length).astype(jnp.float32)
    ones = jnp.ones((chunk, HEAD), jnp.bfloat16)
    order = rotated(blocks)
    place = [order.index(j) for j in range(blocks)]
    to = [lax.rem(z + SPLIT - behind, SPLIT) for z in range(SPLIT)]
    to = [lax.rem(z, SPLIT // 2) * 2 * lines + lax.div(z, SPLIT // 2) for z in to]
    scale = lax.rsqrt(squares_ref[:, :group] / EMBED_DIMENSION + eps_norm)
    scale = jnp.concatenate([scale, jnp.zeros((HEAD - blocks, group), jnp.float32)], axis=0).T
    scales = [jnp.broadcast_to(scale[:, n : n + 1], (group, HEAD)) for n in place]
    product = jnp.zeros((1, 1), jnp.float32)
    squares = jnp.zeros((1, 1), jnp.float32)
    for h in range(heads):
        rows = slice(h * group, (h + 1) * group)
        y = [y_ref[place[j], rows, :].astype(jnp.float32) for j in range(blocks)]
        gain = gain_ref[h : h + 1, :].astype(jnp.float32)
        v = [(y[j] * scales[j] * gain).astype(jnp.bfloat16) for j in range(blocks)]
        v = jnp.concatenate(v, axis=0)
        u = dot(lifting_ref[h], v, ((1,), (1,)))
        query = feature(u[: HEAD // 2]).astype(jnp.bfloat16)
        keys = (feature(u[HEAD // 2 :]) * valid).astype(jnp.bfloat16)
        state = jnp.zeros((HEAD, 2 * HEAD), jnp.float32)
        last = jnp.zeros((1, HEAD), jnp.float32)
        for x in range(lines):
            cut = slice(x * chunk, (x + 1) * chunk)
            q, k = query[:, cut], keys[:, cut]
            wide = jnp.concatenate([v[cut], ones], axis=1)
            a = jnp.where(causal, dot(q, k, ((0,), (0,))), 0.0).astype(jnp.bfloat16)
            both = dot(a, wide, ((1,), (0,)))
            if x:
                high = state.astype(jnp.bfloat16)
                low = (state - high.astype(jnp.float32)).astype(jnp.bfloat16)
                both = both + dot(q, high, ((0,), (0,))) + dot(q, low, ((0,), (0,)))
            out = both[:, :HEAD] / both[:, HEAD:]
            out = out + jnp.concatenate(y[x * SPLIT : (x + 1) * SPLIT], axis=0)
            out = jnp.where(at < length - x * chunk, out, 0.0).astype(jnp.bfloat16)
            for z in range(SPLIT):
                out_ref[to[z] + x * 2, rows, :] = out[z * group : (z + 1) * group]
            out = jnp.where(at == length - 1 - x * chunk, out.astype(jnp.float32), 0.0)
            last = last + jnp.sum(out, axis=0, keepdims=True)
            if x + 1 < lines:
                state = state + dot(k, wide, ((1,), (0,)))
        product = product + jnp.sum(last * readout_ref[h : h + 1, :].astype(jnp.float32), axis=1, keepdims=True)
        squares = squares + jnp.sum(last * last, axis=1, keepdims=True)
    lane = lax.broadcasted_iota(jnp.int32, (EXTRA, HEAD), 1)
    sums = jnp.zeros((EXTRA, HEAD), jnp.float32)
    for n, part in enumerate(three(product) + three(squares)):
        sums = jnp.where(lane == n, part, sums)
    for j in range(blocks):
        out_ref[j, heads * group :, :] = sums.astype(jnp.bfloat16)


def exchanged(pieces, order):
    return lax.all_to_all(
        pieces,
        "ctx",
        split_axis=0,
        concat_axis=0,
        axis_index_groups=[order(lax.axis_size("ctx"))],
        tiled=True,
    )


def vmem():
    return pl.BlockSpec(memory_space=pltpu.VMEM)


def body(
    pending_activity,
    entry_rescale_vector,
    probe_lifting_matrices,
    lookup_lifting_matrices,
    usable_extents,
    payoff_readout_vector,
):
    blocks, sections = lax.axis_size("ctx"), lax.axis_size("pipe")
    group, width = pending_activity.shape[2:]
    y = pending_activity[0, 0]
    probe, lookup = probe_lifting_matrices[0, 0], lookup_lifting_matrices[0, 0]
    heads = probe.shape[0] // blocks
    first = lax.axis_index("ctx") * heads
    lifting = jnp.concatenate([probe.swapaxes(1, 2), lookup.swapaxes(1, 2)], axis=1)
    lifting = lax.dynamic_slice_in_dim(lifting, first, heads)
    gain = lax.dynamic_slice_in_dim(entry_rescale_vector.reshape(-1, HEAD), first, heads)
    readout = lax.dynamic_slice_in_dim(payoff_readout_vector.reshape(-1, HEAD), first, heads)

    squares = pl.pallas_call(
        squares_kernel,
        out_shape=jax.ShapeDtypeStruct((1, group), jnp.float32),
        in_specs=[vmem()],
        out_specs=vmem(),
    )(y)
    squares = lax.psum(squares, "tp")
    turn = squares
    lines, runs, sides, turns = blocks // SPLIT, 4, lax.axis_size("tp"), []
    for dy, dx, dz in TURNS:
        route = [
            (
                ((p * lines + x) * SPLIT + z) * sides + sides - 1,
                (
                    ((p // runs * runs + (p + dy) % runs) * lines + (x + dx) % lines) * SPLIT
                    + (z + dz) % SPLIT
                )
                * sides
                + sides
                - 1,
            )
            for p in range(sections)
            for x in range(lines)
            for z in range(SPLIT)
        ]
        turn = lax.ppermute(turn, ("pipe", "ctx", "tp"), route)
        turns.append(turn)

    shape = (blocks, heads * group + EXTRA, HEAD)
    pieces = pl.pallas_call(
        cut_kernel,
        out_shape=jax.ShapeDtypeStruct(shape, jnp.bfloat16),
        in_specs=[vmem(), vmem()],
        out_specs=vmem(),
    )(y, squares)
    pieces, *turns = lax.optimization_barrier((pieces, *turns))
    pieces = exchanged(pieces, rotated)
    squares = jnp.sum(pieces[:, heads * group : heads * group + 3, :].astype(jnp.float32), axis=1)
    behind = (lax.axis_index("pipe") == sections - 1).astype(jnp.int32)
    out = pl.pallas_call(
        heads_kernel,
        out_shape=jax.ShapeDtypeStruct(shape, jnp.bfloat16),
        in_specs=[pl.BlockSpec(memory_space=pltpu.SMEM)] * 2
        + [vmem()] * 5
        + [pl.BlockSpec(memory_space=pl.ANY)] * len(turns),
        out_specs=vmem(),
        compiler_params=pltpu.CompilerParams(vmem_limit_bytes=32 * 1024 * 1024),
    )(usable_extents, behind.reshape(1, 1), pieces, squares, gain, lifting, readout, *turns)
    out = exchanged(out, ordered)
    sums = jnp.sum(out[:, heads * group, :].astype(jnp.float32), axis=0)
    route = [
        (
            (p * lines + x) * SPLIT + z,
            ((p + 1) % sections * lines + x) * SPLIT + (z + (p + 1) // sections) % SPLIT,
        )
        for p in range(sections)
        for x in range(lines)
        for z in range(SPLIT)
    ]
    handed = lax.ppermute(out, ("pipe", "ctx"), route)
    tiles = handed[:, : heads * group]
    tiles = tiles.reshape(SPLIT // 2, blocks // SPLIT, 2, heads, group // 8, 8, HEAD)
    tiles = tiles.transpose(4, 1, 2, 0, 3, 5, 6).reshape(group // 8, blocks * heads, 8, HEAD)
    tiles = lax.optimization_barrier(tiles)
    handed = tiles.transpose(0, 2, 1, 3).reshape(group, width)
    sums = lax.psum(sums, "tp")
    found = jnp.sum(sums[:3]) * lax.rsqrt(jnp.sum(sums[3:6]) / EMBED_DIMENSION + eps_norm)
    return (handed[None, None], found[None, None])


def solution(mesh):
    placed = (
        P("pipe", None, "ctx", "tp"),
        P("pipe", None, "tp"),
        P("pipe", None, "tp", None, None),
        P("pipe", None, "tp", None, None),
        P("pipe", None),
        P("tp"),
    )
    return jax.shard_map(
        body,
        mesh=mesh,
        in_specs=placed,
        out_specs=(P("pipe", None, "ctx", "tp"), P("pipe", None)),
        check_vma=False,
    )
```
